32 devices in a mesh: ckpt: 2 (over x), fsdp: 8 (over z, y), dp: 2 (over core).
Axes of the slice: x: 2, y: 2, z: 4, core: 2. Of those that a mesh axis runs over, the one named last changes fastest.
Arguments:
- hidden_in: bfloat16 [8, 5120, 1024], P(('ckpt', 'dp'), 'fsdp'), parts along dimension 0, may hold values from -160 to 160, as said below
- cotangent: bfloat16 [8, 5120, 1024], P(('ckpt', 'dp'), 'fsdp'), parts along dimension 0, may hold values from -16 to 16
- context: bfloat16 [8, 2560, 1024], P(('ckpt', 'dp'), 'fsdp'), parts along dimension 0, may hold values from -6 to 6
- norm_gain: bfloat16 [5120], P('fsdp'), may hold values from 0.099609375 to 1.8984375
- signs_rows: int32 [8192], replicated, may hold values 0 or 1
- column_sign_flips: int32 [2048], replicated, may hold values 0 or 1
- kept_index: int32 [16384], replicated, may hold values from 0 to 16777215
Outputs:
- projections: float32 [8, 16384], P(('ckpt', 'dp'), 'fsdp'), parts along dimension 0
The draws below stay inside these ranges and needn't reach their ends.
There are 2 independent parts, one for each index of `ckpt`. The reference program is written for one: setup_inputs(seed, part) draws one part's arguments, and reference() takes and returns one part's arrays. A program takes and returns all parts, laid end to end along the dimension named above; an argument that names none is the same for every part. Nothing has to cross between parts.
Inputs may be any that keep to these rules, and one draw needn't show every extreme that they name: `hidden_in`: each entry is a bfloat16 value of order one to some tens, with token scales that differ from token to token.
All inputs are finite; a program needn't handle non-finite values.
Results may differ from the reference program's by a relative error of at most 0.005.
Values may be sent and summed in bfloat16 or wider, within the bound.
A program may use at most 256 MiB of HBM per device.

```python
import math
import jax
import jax.numpy as jnp
from jax import lax

D = 5120
HC = 2560
ROWS_A = 8192
COLS_B = 2048
PROJ = 16384
SEQ = 1024
EXAMPLES = 4


def common_random_noise(key):
    return jax.random.normal(key, (EXAMPLES, D, SEQ), jnp.float32)


def draw_hidden_in(key, part):
    base = common_random_noise(key)
    key = jax.random.fold_in(key, 3)
    row_key = jax.random.fold_in(key, 0)
    row_scale = jnp.exp(jax.random.uniform(row_key, (EXAMPLES, 1, SEQ), jnp.float32, 0.0, math.log(10.0)))
    column_scale = jnp.exp(jnp.linspace(0.0, math.log(3.0), D, dtype=jnp.float32))
    values = base * row_scale * column_scale[None, :, None]
    values = jnp.clip(values, -160.0, 160.0)
    values = values.at[0, D - 1, 0].set(160.0)
    values = values.at[0, D - 1, 1].set(-160.0)
    return values.astype(jnp.bfloat16)


def draw_cotangent(key, part):
    base = common_random_noise(key)
    key = jax.random.fold_in(key, 5)
    own_noise = jax.random.normal(key, (EXAMPLES, D, SEQ), jnp.float32)
    values = jnp.clip(own_noise + 0.8 * base, -16.0, 16.0)
    return values.astype(jnp.bfloat16)


def plant(array, rng, least, top_value):
    dims = array.shape
    spot = [jax.random.randint(jax.random.fold_in(rng, axis), (), 0, dims[axis]) for axis in range(len(dims))]
    array = array.at[tuple(spot)].set(least)
    longest = dims.index(max(dims))
    spot[longest] = (spot[longest] + 1) % dims[longest]
    return array.at[tuple(spot)].set(top_value)


def block_levels(own_key, dims, pieces, smallest, high):
    def one(dim, shards_of):
        draws = jax.random.uniform(jax.random.fold_in(jax.random.fold_in(own_key, 6), dim), (shards_of,), jnp.float32, smallest / len(pieces), high / len(pieces))
        return jnp.repeat(jnp.exp(draws), dims[dim] // shards_of).reshape((-1,) + (1,) * (len(dims) - dim - 1))

    factor_of = one(*pieces[0])
    for cut in pieces[1:]:
        factor_of = factor_of * one(*cut)
    return factor_of


def scatter_about(stream_key, dims, scale, most, pieces=(), held_as=jnp.bfloat16):
    array = jax.random.normal(stream_key, dims, jnp.float32) * scale
    if len(pieces) > 0:
        array = block_levels(stream_key, dims, pieces, -0.22, 0.18) * array
    return jnp.clip(array, min=-most, max=most).astype(held_as)


def setup_inputs(seed: int = 0, part: int = 0) -> dict:
    keys = jax.random.split(jax.random.key(seed), 8)
    own_keys = jax.random.split(jax.random.fold_in(keys[7], part), 8)
    return {
        "hidden_in": draw_hidden_in(jax.random.fold_in(jax.random.fold_in(keys[7], part), 71), part),
        "cotangent": draw_cotangent(jax.random.fold_in(jax.random.fold_in(keys[7], part), 71), part),
        "context": scatter_about(own_keys[2], (EXAMPLES, HC, SEQ), 1.0, 6.0, ((0, 2), (1, 8))),
        "norm_gain": jnp.clip(1.0 + 0.18 * jax.random.normal(keys[3], (D,), jnp.float32), 0.099609375, 1.8984375).astype(jnp.bfloat16),
        "signs_rows": plant((jax.random.randint(keys[4], (ROWS_A,), 0, 2) < 1).astype(jnp.int32), jax.random.fold_in(keys[4], 1), 0, 1),
        "column_sign_flips": plant((jax.random.randint(keys[5], (COLS_B,), 0, 2) < 1).astype(jnp.int32), jax.random.fold_in(keys[5], 1), 0, 1),
        "kept_index": plant(jax.random.randint(keys[6], (PROJ,), 0, ROWS_A * COLS_B), jax.random.fold_in(keys[6], 1), 0, (ROWS_A * COLS_B) - 1).astype(jnp.int32),
    }


EPS = 1e-06

def bitwise_parity_value(values, bit_count):
    parity_flag = jnp.zeros_like(values)
    for shift_count in range(bit_count):
        parity_flag = parity_flag ^ values >> shift_count & 1
    return parity_flag

def hadamard(order):
    indices = jnp.arange(order, dtype=jnp.int32)
    parity_bits = bitwise_parity_value(indices[:, None] & indices[None, :], order.bit_length())
    return (1 - 2 * parity_bits).astype(jnp.float32)

def rows_transform(values):
    total_rows = values.shape[0]
    low_size = 1 << (total_rows.bit_length() - 1) // 2
    high_size = total_rows // low_size
    sectioned = values.reshape(high_size, low_size, values.shape[1])
    sectioned = jnp.einsum('jb,abc->ajc', hadamard(low_size), sectioned, precision=lax.Precision.HIGHEST)
    sectioned = jnp.einsum('ka,ajc->kjc', hadamard(high_size), sectioned, precision=lax.Precision.HIGHEST)
    return sectioned.reshape(total_rows, values.shape[1])

def reference(hidden_in, cotangent, context, norm_gain, signs_rows, column_sign_flips, kept_index):
    sign_a = (1 - 2 * signs_rows).astype(jnp.float32)
    sign_b = (1 - 2 * column_sign_flips).astype(jnp.float32)
    sign_lookup_matrix = (sign_b[:, None] * hadamard(COLS_B)).astype(jnp.bfloat16)
    live_rows = D * HC // COLS_B
    scale = 1.0 / jnp.sqrt(jnp.float32(ROWS_A * COLS_B * SEQ))
    kept_row = kept_index // COLS_B
    kept_col = kept_index % COLS_B

    def project_one(example):
        hidden_ex, cot_ex, context_ex = example
        hidden = hidden_ex.astype(jnp.float32)
        weighted = norm_gain.astype(jnp.float32)[:, None] * cot_ex.astype(jnp.float32)
        square_sum = lax.optimization_barrier(jnp.sum(hidden * hidden, axis=0))
        cross_sum = lax.optimization_barrier(jnp.sum(weighted * hidden, axis=0))
        inverse = lax.rsqrt(square_sum / D + EPS)
        grad_hidden = (weighted * inverse[None, :] - hidden * (cross_sum * inverse ** 3 / D)[None, :]).astype(jnp.bfloat16)
        gradient_matrix = jnp.dot(grad_hidden, context_ex.T, preferred_element_type=jnp.float32).astype(jnp.bfloat16)
        live = gradient_matrix.reshape(live_rows, COLS_B)
        mixed_live = jnp.dot(live, sign_lookup_matrix, preferred_element_type=jnp.float32).astype(jnp.bfloat16)
        mixed_rows = jnp.concatenate([mixed_live, jnp.zeros((ROWS_A - live_rows, COLS_B), jnp.bfloat16)], axis=0)
        full = rows_transform(mixed_rows.astype(jnp.float32) * sign_a[:, None])
        return full[kept_row, kept_col] * scale
    return lax.map(project_one, (hidden_in, cotangent, context))
```

```python
import functools
import math

import jax
import jax.numpy as jnp
import numpy as np
from jax import lax
from jax.experimental import pallas as pl
from jax.experimental.pallas import tpu as pltpu
from jax.sharding import PartitionSpec as P

EPS = 1e-06
GROUPS = 50
HALF = 64
SEG = 512
LOW = 256
NT = (((1,), (1,)), ((), ()))


def hadamard_np(order):
    h = np.ones((1, 1), np.float32)
    while h.shape[0] < order:
        h = np.block([[h, h], [h, -h]])
    return h


def parity(values):
    for shift in (8, 4, 2, 1):
        values = values ^ (values >> shift)
    return values & 1


def dot_nt(a, b):
    return lax.dot_general(a, b, NT, preferred_element_type=jnp.float32)


def project_kernel(
    low_rows, cols, span, row_pad, pos_ref, kept_ref, kept_rows_ref, g_ref, c_ref, b_ref, l_ref, h_ref, eye_ref,
    out_ref, x_ref, table_ref, buf_ref,
):
    segs = c_ref.shape[1] // SEG
    parts = cols // SEG
    for e in range(2):
        for nb in range(segs):
            block = dot_nt(g_ref[e], c_ref[e, nb * SEG : (nb + 1) * SEG, :])
            for gamma in range(parts):
                omega, sigma = divmod(segs * gamma + nb, parts)
                signed = block[gamma * row_pad : (gamma + 1) * row_pad] * b_ref[0:1, sigma * SEG : (sigma + 1) * SEG]
                x_ref[e, omega * row_pad : (omega + 1) * row_pad, sigma * SEG : (sigma + 1) * SEG] = signed.astype(
                    jnp.bfloat16
                )
    per_step = min(low_rows, 4)
    high = cols // LOW

    def table_step(step, carry):
        start = pl.multiple_of(step * (per_step * HALF), per_step * HALF)
        mixed = []
        for e in range(2):
            t = jnp.dot(l_ref[pl.ds(start, per_step * HALF), :], x_ref[e], preferred_element_type=jnp.float32)
            blocks = [t[:, h * LOW : (h + 1) * LOW] for h in range(high)]
            width = 1
            while width < high:
                new = list(blocks)
                for h in range(high):
                    if h & width == 0:
                        new[h] = blocks[h] + blocks[h | width]
                        new[h | width] = blocks[h] - blocks[h | width]
                blocks = new
                width *= 2
            mixed.append([v.astype(jnp.bfloat16) for v in blocks])
        for h in range(high):
            y = jnp.concatenate(
                [mixed[e][h][p * HALF : (p + 1) * HALF] for p in range(per_step) for e in range(2)], axis=0
            )
            r = dot_nt(h_ref[...], y)
            for p in range(per_step):
                row = pl.multiple_of((step * per_step + p) * cols + h * LOW, LOW)
                table_ref[pl.ds(row, LOW), :] = r[:, p * 2 * HALF : (p + 1) * 2 * HALF]
        return carry

    lax.fori_loop(0, low_rows // per_step, table_step, 0)

    shift = (low_rows * cols).bit_length() - 1
    mask = low_rows * cols - 1
    first_group = pos_ref[0] * GROUPS
    unroll = 32

    def pick_step(chunk, carry):
        def rows(group, inner):
            base = pl.multiple_of(group * unroll, unroll)
            for u in range(unroll):
                index = kept_ref[chunk * span + base + u] & mask
                buf_ref[pl.ds(base + u, 1), :] = table_ref[pl.ds(index, 1), :]
            return inner

        lax.fori_loop(0, span // unroll, rows, 0)
        values = buf_ref[...]
        upper = values.astype(jnp.bfloat16)
        lower = (values - upper.astype(jnp.float32)).astype(jnp.bfloat16)
        turned = dot_nt(eye_ref[...], upper) + dot_nt(eye_ref[...], lower)
        kept_high = kept_rows_ref[pl.ds(chunk, 1), :] >> shift
        group_index = lax.broadcasted_iota(jnp.int32, (HALF, span), 0) + first_group
        sign = (1 - 2 * parity(group_index & kept_high)).astype(jnp.float32)
        for e in range(2):
            total = jnp.sum(turned[e * HALF : (e + 1) * HALF] * sign, axis=0, keepdims=True)
            out_ref[chunk, e : e + 1, :] = total
        return carry

    lax.fori_loop(0, kept_rows_ref.shape[0], pick_step, 0)


def scatter_kernel(n, scale, in_ref, out_ref, land_ref, send_sem, recv_sem):
    me = lax.axis_index("fsdp")
    barrier = pltpu.get_barrier_semaphore()
    for k in range(1, n):
        pl.semaphore_signal(
            barrier, inc=1, device_id={"fsdp": lax.rem(me + k, n)}, device_id_type=pl.DeviceIdType.MESH
        )
    pl.semaphore_wait(barrier, n - 1)
    copies = []
    for k in range(1, n):
        peer = lax.rem(me + k, n)
        copy = pltpu.make_async_remote_copy(
            src_ref=in_ref.at[peer],
            dst_ref=land_ref.at[k - 1],
            send_sem=send_sem.at[k - 1],
            recv_sem=recv_sem.at[k - 1],
            device_id={"fsdp": peer},
            device_id_type=pl.DeviceIdType.MESH,
        )
        copy.start()
        copies.append(copy)
    total = in_ref[me]
    for k, copy in enumerate(copies):
        copy.wait()
        total = total + land_ref[k]
    out_ref[...] = total * scale


def on_device(n, hidden_in, cotangent, context, norm_gain, signs_rows, column_sign_flips, kept_index):
    pos = lax.axis_index("fsdp")
    examples, local_d, seq = hidden_in.shape
    d_total = local_d * n
    rows_a, cols, kept = signs_rows.shape[0], column_sign_flips.shape[0], kept_index.shape[0]
    hc = context.shape[1] * n
    local_rows = local_d * hc // cols
    low_rows = local_rows // GROUPS
    parts, segs = cols // SEG, hc // SEG
    deltas = local_d // parts
    row_pad = -(-deltas // 16) * 16

    hidden = hidden_in.astype(jnp.float32)
    weighted = norm_gain.astype(jnp.float32)[None, :, None] * cotangent.astype(jnp.float32)
    square_sum, cross_sum = lax.psum(
        (jnp.sum(hidden * hidden, axis=1), jnp.sum(weighted * hidden, axis=1)), "fsdp"
    )
    inverse = lax.rsqrt(square_sum / d_total + EPS)
    grad_hidden = (
        weighted * inverse[:, None, :] - hidden * (cross_sum * inverse**3 / d_total)[:, None, :]
    ).astype(jnp.bfloat16)
    g = grad_hidden.reshape(examples, deltas, parts, seq).transpose(0, 2, 1, 3)
    g = jnp.pad(g, ((0, 0), (0, 0), (0, row_pad - deltas), (0, 0))).reshape(examples, parts * row_pad, seq)
    full_context = lax.all_gather(context, "fsdp", axis=1, tiled=True)

    sign_b = (1 - 2 * column_sign_flips).astype(jnp.float32)[None, :]
    delta = np.arange(row_pad)
    w = segs * delta[None, :] + np.arange(segs)[:, None]
    live = np.broadcast_to(delta[None, :] < deltas, w.shape).reshape(-1)
    w = np.where(live, w.reshape(-1), 0)
    local_flips = lax.dynamic_slice_in_dim(signs_rows, pos * local_rows, local_rows, 0)
    flips = local_flips.reshape(deltas, segs).T
    flips = jnp.pad(flips, ((0, 0), (0, row_pad - deltas))).reshape(-1)
    sign_a = (1 - 2 * flips).astype(jnp.bfloat16)
    ham = hadamard_np(low_rows)[:, w % low_rows]
    member = (np.arange(HALF)[:, None] == (w // low_rows)[None, :]) & live[None, :]
    l = (ham[:, None, :] * member[None, :, :]).reshape(low_rows * HALF, segs * row_pad)
    l = jnp.asarray(l.astype(np.int8)).astype(jnp.bfloat16) * sign_a[None, :]

    span = min(512, kept // n)
    chunks = kept // span
    vmem = pl.BlockSpec(memory_space=pltpu.VMEM)
    smem = pl.BlockSpec(memory_space=pltpu.SMEM)
    partial = pl.pallas_call(
        functools.partial(project_kernel, low_rows, cols, span, row_pad),
        out_shape=jax.ShapeDtypeStruct((chunks, 2, span), jnp.float32),
        in_specs=[smem, smem] + [vmem] * 7,
        out_specs=vmem,
        scratch_shapes=[
            pltpu.VMEM((2, segs * row_pad, cols), jnp.bfloat16),
            pltpu.VMEM((low_rows * cols, 2 * HALF), jnp.float32),
            pltpu.VMEM((span, 2 * HALF), jnp.float32),
        ],
        compiler_params=pltpu.CompilerParams(vmem_limit_bytes=58 * 2**20),
        name="project",
    )(
        pos.reshape(1),
        kept_index,
        kept_index.reshape(chunks, span),
        g,
        full_context,
        sign_b,
        l,
        jnp.asarray(hadamard_np(LOW), jnp.bfloat16),
        jnp.eye(2 * HALF, dtype=jnp.bfloat16),
    )
    own = chunks // n
    scale = 1.0 / math.sqrt(rows_a * cols * seq)
    total = pl.pallas_call(
        functools.partial(scatter_kernel, n, scale),
        out_shape=jax.ShapeDtypeStruct((own * 2, span), jnp.float32),
        in_specs=[vmem],
        out_specs=vmem,
        scratch_shapes=[
            pltpu.VMEM((n - 1, own * 2, span), jnp.float32),
            pltpu.SemaphoreType.DMA((n - 1,)),
            pltpu.SemaphoreType.DMA((n - 1,)),
        ],
        compiler_params=pltpu.CompilerParams(collective_id=0, has_side_effects=True),
        name="scatter_sum",
    )(partial.reshape(n, own * 2, span))
    return total.reshape(own, 2, span).transpose(1, 0, 2).reshape(2, own * span)


def solution(mesh):
    return jax.shard_map(
        functools.partial(on_device, mesh.shape["fsdp"]),
        mesh=mesh,
        in_specs=(
            P(("ckpt", "dp"), "fsdp", None),
            P(("ckpt", "dp"), "fsdp", None),
            P(("ckpt", "dp"), "fsdp", None),
            P("fsdp"),
            P(),
            P(),
            P(),
        ),
        out_specs=P(("ckpt", "dp"), "fsdp"),
        check_vma=False,
    )
```

```python
import functools
import math

import jax
import jax.numpy as jnp
import numpy as np
from jax import lax
from jax.experimental import pallas as pl
from jax.experimental.pallas import tpu as pltpu
from jax.sharding import PartitionSpec as P

EPS = 1e-06
GROUPS = 50
HALF = 64
SEG = 512
LOW = 256
NT = (((1,), (1,)), ((), ()))


def hadamard_np(order):
    h = np.ones((1, 1), np.float32)
    while h.shape[0] < order:
        h = np.block([[h, h], [h, -h]])
    return h


def parity(values):
    for shift in (8, 4, 2, 1):
        values = values ^ (values >> shift)
    return values & 1


def dot_nt(a, b):
    return lax.dot_general(a, b, NT, preferred_element_type=jnp.float32)


def project_kernel(
    low_rows, cols, span, row_pad, pos_ref, kept_ref, kept_rows_ref, g_ref, c_ref, b_ref, l_ref, h_ref, eye_ref,
    out_ref, x_ref, table_ref, buf_ref,
):
    segs = c_ref.shape[0] // SEG
    parts = cols // SEG
    for e in range(2):
        for nb in range(segs):
            block = dot_nt(g_ref[e], c_ref[nb * SEG : (nb + 1) * SEG, :])
            for gamma in range(parts):
                omega, sigma = divmod(segs * gamma + nb, parts)
                signed = block[gamma * row_pad : (gamma + 1) * row_pad] * b_ref[0:1, sigma * SEG : (sigma + 1) * SEG]
                x_ref[e, omega * row_pad : (omega + 1) * row_pad, sigma * SEG : (sigma + 1) * SEG] = signed.astype(
                    jnp.bfloat16
                )
    per_step = min(low_rows, 4)
    high = cols // LOW

    def table_step(step, carry):
        start = pl.multiple_of(step * (per_step * HALF), per_step * HALF)
        mixed = []
        for e in range(2):
            t = jnp.dot(l_ref[e, pl.ds(start, per_step * HALF), :], x_ref[e], preferred_element_type=jnp.float32)
            blocks = [t[:, h * LOW : (h + 1) * LOW] for h in range(high)]
            width = 1
            while width < high:
                new = list(blocks)
                for h in range(high):
                    if h & width == 0:
                        new[h] = blocks[h] + blocks[h | width]
                        new[h | width] = blocks[h] - blocks[h | width]
                blocks = new
                width *= 2
            mixed.append([v.astype(jnp.bfloat16) for v in blocks])
        for h in range(high):
            y = jnp.concatenate(
                [mixed[e][h][p * HALF : (p + 1) * HALF] for p in range(per_step) for e in range(2)], axis=0
            )
            r = dot_nt(h_ref[...], y)
            for p in range(per_step):
                row = pl.multiple_of((step * per_step + p) * cols + h * LOW, LOW)
                table_ref[pl.ds(row, LOW), :] = r[:, p * 2 * HALF : (p + 1) * 2 * HALF]
        return carry

    lax.fori_loop(0, low_rows // per_step, table_step, 0)

    shift = (low_rows * cols).bit_length() - 1
    mask = low_rows * cols - 1
    first_group = pos_ref[0] * GROUPS
    unroll = 32

    def pick_step(chunk, carry):
        def rows(group, inner):
            base = pl.multiple_of(group * unroll, unroll)
            for u in range(unroll):
                index = kept_ref[chunk * span + base + u] & mask
                buf_ref[pl.ds(base + u, 1), :] = table_ref[pl.ds(index, 1), :]
            return inner

        lax.fori_loop(0, span // unroll, rows, 0)
        values = buf_ref[...]
        upper = values.astype(jnp.bfloat16)
        lower = (values - upper.astype(jnp.float32)).astype(jnp.bfloat16)
        turned = dot_nt(eye_ref[...], upper) + dot_nt(eye_ref[...], lower)
        kept_high = kept_rows_ref[pl.ds(chunk, 1), :] >> shift
        lane = lax.broadcasted_iota(jnp.int32, (2 * HALF, span), 0)
        group_index = first_group + jnp.where(lane >= HALF, lane + (GROUPS - HALF), lane)
        sign = (1 - 2 * parity(group_index & kept_high)).astype(jnp.float32)
        own = out_ref.shape[1]
        out_ref[chunk // own, pl.ds(lax.rem(chunk, own), 1), :] = jnp.sum(turned * sign, axis=0, keepdims=True)
        return carry

    lax.fori_loop(0, kept_rows_ref.shape[0], pick_step, 0)


def greet(n, me):
    barrier = pltpu.get_barrier_semaphore()
    for k in range(1, n):
        pl.semaphore_signal(
            barrier, inc=1, device_id={"fsdp": lax.rem(me + k, n)}, device_id_type=pl.DeviceIdType.MESH
        )
    pl.semaphore_wait(barrier, n - 1)


def remote(src, dst, send_sem, recv_sem, peer):
    return pltpu.make_async_remote_copy(
        src_ref=src,
        dst_ref=dst,
        send_sem=send_sem,
        recv_sem=recv_sem,
        device_id={"fsdp": peer},
        device_id_type=pl.DeviceIdType.MESH,
    )


def exchange_kernel(
    n, d_total, row_pad, hidden_ref, cot_ref, gain_ref, context_ref, c_ref, g_ref,
    stats_ref, whole_ref, land_ref, stage_ref, gbuf_ref,
    stat_send, stat_recv, pair_send, pair_recv, right_send, right_recv, left_send, left_recv, local_sem,
):
    me = lax.axis_index("fsdp")
    y = lax.rem(me, 2)
    z = me // 2
    nz = n // 2
    partner = me + 1 - 2 * y
    local_d, seq = hidden_ref.shape[1:]
    parts = gbuf_ref.shape[1] // row_pad
    greet(n, me)

    def right(step, sub):
        half = y if sub == 0 else 1 - y
        block = lax.max(z - step, 0)
        src = context_ref.at[y] if step == 0 and sub == 0 else c_ref.at[block, half]
        return remote(
            src, c_ref.at[block, half], right_send.at[step, sub], right_recv.at[step, sub], lax.min(me + 2, n - 1)
        )

    def left(step, sub):
        half = y if sub == 0 else 1 - y
        block = lax.min(z + step, nz - 1)
        src = context_ref.at[y] if step == 0 and sub == 0 else c_ref.at[block, half]
        return remote(
            src, c_ref.at[block, half], left_send.at[step, sub], left_recv.at[step, sub], lax.max(me - 2, 0)
        )

    def sends_right(step):
        return jnp.logical_and(z < nz - 1, z >= step)

    def sends_left(step):
        return jnp.logical_and(z > 0, z + step < nz)

    def start_both(step, sub):
        @pl.when(sends_right(step))
        def _():
            right(step, sub).start()

        @pl.when(sends_left(step))
        def _():
            left(step, sub).start()

    swap = remote(context_ref.at[1 - y], c_ref.at[z, y], pair_send.at[0], pair_recv.at[0], partner)
    swap.start()
    start_both(0, 0)
    keep = pltpu.make_async_copy(context_ref.at[y], c_ref.at[z, y], local_sem.at[0])
    keep.start()

    rows = 32

    def add_rows(tile, carry):
        start = pl.multiple_of(tile * rows, rows)
        gain = gain_ref[pl.ds(start, rows), :]
        out = []
        for e in range(2):
            h = hidden_ref[e, pl.ds(start, rows), :].astype(jnp.float32)
            w = cot_ref[e, pl.ds(start, rows), :].astype(jnp.float32) * gain
            out.append(carry[2 * e] + jnp.sum((h * h).reshape(rows // 8, 8, seq), axis=0))
            out.append(carry[2 * e + 1] + jnp.sum((w * h).reshape(rows // 8, 8, seq), axis=0))
        return tuple(out)

    sums = lax.fori_loop(0, local_d // rows, add_rows, (jnp.zeros((8, seq), jnp.float32),) * 4)
    for k in range(4):
        stats_ref[k : k + 1, :] = jnp.sum(sums[k], axis=0, keepdims=True)
    stats_ref[4:8, :] = jnp.zeros((4, seq), jnp.float32)
    stat_copies = []
    for k in range(1, n):
        copy = remote(
            stats_ref, land_ref.at[k], stat_send.at[k], stat_recv.at[k], lax.rem(me + k, n)
        )
        copy.start()
        stat_copies.append(copy)
    swap.wait_recv()
    start_both(0, 1)
    land_ref[0] = stats_ref[...]
    for copy in stat_copies:
        copy.wait_recv()
    total = land_ref[0]
    for k in range(1, n):
        total = total + land_ref[k]
    for copy in stat_copies:
        copy.wait_send()
    for k in range(4):
        whole_ref[k] = total[k : k + 1, :]

    stage_ref[...] = jnp.zeros_like(stage_ref)

    def gradient_of(e, slot):
        def tokens(tile, carry):
            lanes = pl.ds(pl.multiple_of(tile * 128, 128), 128)
            inverse = lax.rsqrt(whole_ref[2 * e, :, lanes] / d_total + EPS)
            factor = whole_ref[2 * e + 1, :, lanes] * inverse * inverse * inverse / d_total
            h = hidden_ref[e, :, lanes].astype(jnp.float32)
            w = cot_ref[e, :, lanes].astype(jnp.float32) * gain_ref[...]
            stage_ref[0:local_d, :] = w * inverse - h * factor
            for gamma in range(parts):
                picked = stage_ref[pl.ds(gamma, row_pad, stride=parts), :]
                gbuf_ref[slot, gamma * row_pad : (gamma + 1) * row_pad, lanes] = picked.astype(jnp.bfloat16)
            return carry

        lax.fori_loop(0, seq // 128, tokens, 0)

    gradient_of(1 - y, 0)
    give = remote(gbuf_ref.at[0], g_ref.at[y], pair_send.at[1], pair_recv.at[1], partner)
    give.start()
    gradient_of(y, 1)
    hold = pltpu.make_async_copy(gbuf_ref.at[1], g_ref.at[y], local_sem.at[1])
    hold.start()

    for step in range(nz - 1):
        for sub in range(2):
            @pl.when(z >= step + 1)
            def _():
                right(step, sub).wait_recv()

            @pl.when(z + step + 1 < nz)
            def _():
                left(step, sub).wait_recv()

            if step + 1 < nz - 1:
                start_both(step + 1, sub)
    for step in range(nz - 1):
        for sub in range(2):

            @pl.when(sends_right(step))
            def _():
                right(step, sub).wait_send()

            @pl.when(sends_left(step))
            def _():
                left(step, sub).wait_send()

    swap.wait_send()
    keep.wait()
    give.wait()
    hold.wait()


def scatter_kernel(n, scale, in_ref, out_ref, land_ref, send_sem, recv_sem):
    me = lax.axis_index("fsdp")
    y = lax.rem(me, 2)
    greet(n, me)
    copies = []
    for k in range(1, n):
        peer = lax.rem(me + k, n)
        copy = remote(in_ref.at[peer], land_ref.at[k - 1], send_sem.at[k - 1], recv_sem.at[k - 1], peer)
        copy.start()
        copies.append(copy)
    totals = [in_ref[me], None]
    for k in range(1, n):
        copies[k - 1].wait()
        value = land_ref[k - 1]
        totals[k % 2] = value if totals[k % 2] is None else totals[k % 2] + value
    out_ref[y] = totals[0] * scale
    out_ref[1 - y] = totals[1] * scale


def on_device(n, hidden_in, cotangent, context, norm_gain, signs_rows, column_sign_flips, kept_index):
    pos = lax.axis_index("fsdp")
    local_d, seq = hidden_in.shape[1:]
    d_total = local_d * n
    rows_a, cols, kept = signs_rows.shape[0], column_sign_flips.shape[0], kept_index.shape[0]
    local_hc = context.shape[1]
    hc = local_hc * n
    local_rows = local_d * hc // cols
    low_rows = local_rows // GROUPS
    parts, segs = cols // SEG, hc // SEG
    deltas = local_d // parts
    row_pad = -(-deltas // 16) * 16
    vmem = pl.BlockSpec(memory_space=pltpu.VMEM)
    smem = pl.BlockSpec(memory_space=pltpu.SMEM)
    anywhere = pl.BlockSpec(memory_space=pl.ANY)
    dma = pltpu.SemaphoreType.DMA
    nz = n // 2

    full_context, g = pl.pallas_call(
        functools.partial(exchange_kernel, n, d_total, row_pad),
        out_shape=(
            jax.ShapeDtypeStruct((nz, 2, local_hc, seq), jnp.bfloat16),
            jax.ShapeDtypeStruct((2, parts * row_pad, seq), jnp.bfloat16),
        ),
        in_specs=[vmem, vmem, vmem, anywhere],
        out_specs=(anywhere, anywhere),
        scratch_shapes=[
            pltpu.VMEM((8, seq), jnp.float32),
            pltpu.VMEM((4, 1, seq), jnp.float32),
            pltpu.VMEM((n, 8, seq), jnp.float32),
            pltpu.VMEM((parts * row_pad, 128), jnp.float32),
            pltpu.VMEM((2, parts * row_pad, seq), jnp.bfloat16),
            dma((n,)),
            dma((n,)),
            dma((2,)),
            dma((2,)),
            dma((nz - 1, 2)),
            dma((nz - 1, 2)),
            dma((nz - 1, 2)),
            dma((nz - 1, 2)),
            dma((2,)),
        ],
        compiler_params=pltpu.CompilerParams(
            collective_id=1, has_side_effects=True, vmem_limit_bytes=40 * 2**20
        ),
        name="exchange",
    )(hidden_in, cotangent, norm_gain.astype(jnp.float32)[:, None], context)

    sign_b = (1 - 2 * column_sign_flips).astype(jnp.float32)[None, :]
    delta = np.arange(row_pad)
    w = segs * delta[None, :] + np.arange(segs)[:, None]
    live = np.broadcast_to(delta[None, :] < deltas, w.shape).reshape(-1)
    w = np.where(live, w.reshape(-1), 0)
    pair_flips = lax.dynamic_slice_in_dim(signs_rows, (pos // 2) * (2 * local_rows), 2 * local_rows, 0)
    flips = pair_flips.reshape(2, deltas, segs).transpose(0, 2, 1)
    flips = jnp.pad(flips, ((0, 0), (0, 0), (0, row_pad - deltas))).reshape(2, 1, -1)
    sign_a = (1 - 2 * flips).astype(jnp.bfloat16)
    ham = hadamard_np(low_rows)[:, w % low_rows]
    member = (np.arange(HALF)[:, None] == (w // low_rows)[None, :]) & live[None, :]
    l = (ham[:, None, :] * member[None, :, :]).reshape(low_rows * HALF, segs * row_pad)
    l = jnp.asarray(l.astype(np.int8)).astype(jnp.bfloat16)[None] * sign_a

    span = min(512, kept // n)
    chunks = kept // span
    own = chunks // n
    partial = pl.pallas_call(
        functools.partial(project_kernel, low_rows, cols, span, row_pad),
        out_shape=jax.ShapeDtypeStruct((n, own, span), jnp.float32),
        in_specs=[smem, smem] + [vmem] * 7,
        out_specs=vmem,
        scratch_shapes=[
            pltpu.VMEM((2, segs * row_pad, cols), jnp.bfloat16),
            pltpu.VMEM((low_rows * cols, 2 * HALF), jnp.float32),
            pltpu.VMEM((span, 2 * HALF), jnp.float32),
        ],
        compiler_params=pltpu.CompilerParams(vmem_limit_bytes=58 * 2**20),
        name="project",
    )(
        (pos // 2 * 2).reshape(1),
        kept_index,
        kept_index.reshape(chunks, span),
        g,
        full_context.reshape(hc, seq),
        sign_b,
        l,
        jnp.asarray(hadamard_np(LOW), jnp.bfloat16),
        jnp.eye(2 * HALF, dtype=jnp.bfloat16),
    )
    scale = 1.0 / math.sqrt(rows_a * cols * seq)
    total = pl.pallas_call(
        functools.partial(scatter_kernel, n, scale),
        out_shape=jax.ShapeDtypeStruct((2, own, span), jnp.float32),
        in_specs=[vmem],
        out_specs=vmem,
        scratch_shapes=[pltpu.VMEM((n - 1, own, span), jnp.float32), dma((n - 1,)), dma((n - 1,))],
        compiler_params=pltpu.CompilerParams(collective_id=0, has_side_effects=True),
        name="scatter_sum",
    )(partial)
    return total.reshape(2, own * span)


def solution(mesh):
    return jax.shard_map(
        functools.partial(on_device, mesh.shape["fsdp"]),
        mesh=mesh,
        in_specs=(
            P(("ckpt", "dp"), "fsdp", None),
            P(("ckpt", "dp"), "fsdp", None),
            P(("ckpt", "dp"), "fsdp", None),
            P("fsdp"),
            P(),
            P(),
            P(),
        ),
        out_specs=P(("ckpt", "dp"), "fsdp"),
        check_vma=False,
    )
```

```python
import functools
import math

import jax
import jax.numpy as jnp
import numpy as np
from jax import lax
from jax.experimental import pallas as pl
from jax.experimental.pallas import tpu as pltpu
from jax.sharding import PartitionSpec as P

EPS = 1e-06
GROUPS = 50
HALF = 64
SEG = 512
LOW = 256
NT = (((1,), (1,)), ((), ()))


def hadamard_np(order):
    h = np.ones((1, 1), np.float32)
    while h.shape[0] < order:
        h = np.block([[h, h], [h, -h]])
    return h


def parity(values):
    for shift in (8, 4, 2, 1):
        values = values ^ (values >> shift)
    return values & 1


def dot_nt(a, b):
    return lax.dot_general(a, b, NT, preferred_element_type=jnp.float32)


def project_kernel(
    low_rows, cols, span, row_pad, pos_ref, kept_ref, kept_rows_ref, g_ref, c_ref, b_ref, a_ref, l_ref, h_ref, eye_ref,
    out_ref, x_ref, table_ref, even_ref, odd_ref,
):
    segs = c_ref.shape[0] // SEG
    parts = cols // SEG
    for e in range(2):
        for nb in range(segs):
            block = dot_nt(g_ref[e], c_ref[nb * SEG : (nb + 1) * SEG, :])
            for gamma in range(parts):
                omega, sigma = divmod(segs * gamma + nb, parts)
                signed = block[gamma * row_pad : (gamma + 1) * row_pad] * b_ref[0:1, sigma * SEG : (sigma + 1) * SEG]
                x_ref[e, omega * row_pad : (omega + 1) * row_pad, sigma * SEG : (sigma + 1) * SEG] = signed.astype(
                    jnp.bfloat16
                )
    per_step = min(low_rows, 4)
    high = cols // LOW

    def table_step(step, carry):
        start = pl.multiple_of(step * (per_step * HALF), per_step * HALF)
        mixed = []
        for e in range(2):
            left = l_ref[pl.ds(start, per_step * HALF), :] * a_ref[e]
            t = jnp.dot(left, x_ref[e], preferred_element_type=jnp.float32)
            blocks = [t[:, h * LOW : (h + 1) * LOW] for h in range(high)]
            width = 1
            while width < high:
                new = list(blocks)
                for h in range(high):
                    if h & width == 0:
                        new[h] = blocks[h] + blocks[h | width]
                        new[h | width] = blocks[h] - blocks[h | width]
                blocks = new
                width *= 2
            mixed.append([v.astype(jnp.bfloat16) for v in blocks])
        for h in range(high):
            y = jnp.concatenate(
                [mixed[e][h][p * HALF : (p + 1) * HALF] for p in range(per_step) for e in range(2)], axis=0
            )
            r = dot_nt(h_ref[...], y)
            for p in range(per_step):
                row = pl.multiple_of((step * per_step + p) * cols + h * LOW, LOW)
                table_ref[pl.ds(row, LOW), :] = r[:, p * 2 * HALF : (p + 1) * 2 * HALF]
        return carry

    lax.fori_loop(0, low_rows // per_step, table_step, 0)

    shift = (low_rows * cols).bit_length() - 1
    mask = low_rows * cols - 1
    first_group = pos_ref[0] * GROUPS
    own = out_ref.shape[1]
    chunks = kept_rows_ref.shape[0]

    def pick(chunk, buf_ref):
        base = pl.multiple_of(chunk * span, span)
        for u in range(span):
            index = kept_ref[base + u] & mask
            buf_ref[u : u + 1, :] = table_ref[pl.ds(index, 1), :]

    def sign_sum(chunk, buf_ref):
        values = buf_ref[...]
        upper = values.astype(jnp.bfloat16)
        lower = (values - upper.astype(jnp.float32)).astype(jnp.bfloat16)
        turned = dot_nt(eye_ref[...], upper) + dot_nt(eye_ref[...], lower)
        kept_high = kept_rows_ref[pl.ds(chunk, 1), :] >> shift
        lane = lax.broadcasted_iota(jnp.int32, (2 * HALF, span), 0)
        group_index = first_group + jnp.where(lane >= HALF, lane + (GROUPS - HALF), lane)
        sign = (1 - 2 * parity(group_index & kept_high)).astype(jnp.float32)
        out_ref[chunk // own, pl.ds(lax.rem(chunk, own), 1), :] = jnp.sum(turned * sign, axis=0, keepdims=True)

    odd_ref[...] = jnp.zeros_like(odd_ref)

    def pick_step(step, carry):
        pick(2 * step, even_ref)
        sign_sum(lax.max(2 * step - 1, 0), odd_ref)
        pick(2 * step + 1, odd_ref)
        sign_sum(2 * step, even_ref)
        return carry

    lax.fori_loop(0, chunks // 2, pick_step, 0)
    sign_sum(chunks - 1, odd_ref)


def greet(n, me):
    barrier = pltpu.get_barrier_semaphore()
    for k in range(1, n):
        pl.semaphore_signal(
            barrier, inc=1, device_id={"fsdp": lax.rem(me + k, n)}, device_id_type=pl.DeviceIdType.MESH
        )
    pl.semaphore_wait(barrier, n - 1)


def remote(src, dst, send_sem, recv_sem, peer):
    return pltpu.make_async_remote_copy(
        src_ref=src,
        dst_ref=dst,
        send_sem=send_sem,
        recv_sem=recv_sem,
        device_id={"fsdp": peer},
        device_id_type=pl.DeviceIdType.MESH,
    )


def exchange_kernel(
    n, d_total, row_pad, hidden_in_ref, cot_in_ref, gain_ref, context_ref, c_ref, g_ref,
    hidden_ref, cot_ref, stats_ref, whole_ref, land_ref, stage_ref, gbuf_ref,
    stat_send, stat_recv, pair_send, pair_recv, right_send, right_recv, left_send, left_recv, local_sem,
):
    me = lax.axis_index("fsdp")
    y = lax.rem(me, 2)
    z = me // 2
    nz = n // 2
    partner = me + 1 - 2 * y
    local_d, seq = hidden_ref.shape[1:]
    parts = gbuf_ref.shape[1] // row_pad
    reads = [
        pltpu.make_async_copy(hidden_in_ref, hidden_ref, local_sem.at[2]),
        pltpu.make_async_copy(cot_in_ref, cot_ref, local_sem.at[3]),
    ]
    for read in reads:
        read.start()
    greet(n, me)

    def right(step, sub):
        half = y if sub == 0 else 1 - y
        block = lax.max(z - step, 0)
        src = context_ref.at[y] if step == 0 and sub == 0 else c_ref.at[block, half]
        return remote(
            src, c_ref.at[block, half], right_send.at[step, sub], right_recv.at[step, sub], lax.min(me + 2, n - 1)
        )

    def left(step, sub):
        half = y if sub == 0 else 1 - y
        block = lax.min(z + step, nz - 1)
        src = context_ref.at[y] if step == 0 and sub == 0 else c_ref.at[block, half]
        return remote(
            src, c_ref.at[block, half], left_send.at[step, sub], left_recv.at[step, sub], lax.max(me - 2, 0)
        )

    def sends_right(step):
        return jnp.logical_and(z < nz - 1, z >= step)

    def sends_left(step):
        return jnp.logical_and(z > 0, z + step < nz)

    def start_both(step, sub):
        @pl.when(sends_right(step))
        def _():
            right(step, sub).start()

        @pl.when(sends_left(step))
        def _():
            left(step, sub).start()

    swap = remote(context_ref.at[1 - y], c_ref.at[z, y], pair_send.at[0], pair_recv.at[0], partner)
    swap.start()
    start_both(0, 0)
    keep = pltpu.make_async_copy(context_ref.at[y], c_ref.at[z, y], local_sem.at[0])
    keep.start()
    for read in reads:
        read.wait()

    rows = 32

    def add_rows(tile, carry):
        start = pl.multiple_of(tile * rows, rows)
        gain = gain_ref[pl.ds(start, rows), :]
        out = []
        for e in range(2):
            h = hidden_ref[e, pl.ds(start, rows), :].astype(jnp.float32)
            w = cot_ref[e, pl.ds(start, rows), :].astype(jnp.float32) * gain
            out.append(carry[2 * e] + jnp.sum((h * h).reshape(rows // 8, 8, seq), axis=0))
            out.append(carry[2 * e + 1] + jnp.sum((w * h).reshape(rows // 8, 8, seq), axis=0))
        return tuple(out)

    sums = lax.fori_loop(0, local_d // rows, add_rows, (jnp.zeros((8, seq), jnp.float32),) * 4)
    for k in range(4):
        stats_ref[k : k + 1, :] = jnp.sum(sums[k], axis=0, keepdims=True)
    stats_ref[4:8, :] = jnp.zeros((4, seq), jnp.float32)
    stat_copies = []
    for k in range(1, n):
        copy = remote(
            stats_ref, land_ref.at[k], stat_send.at[k], stat_recv.at[k], lax.rem(me + k, n)
        )
        copy.start()
        stat_copies.append(copy)
    swap.wait_recv()
    start_both(0, 1)
    land_ref[0] = stats_ref[...]
    for copy in stat_copies:
        copy.wait_recv()
    total = land_ref[0]
    for k in range(1, n):
        total = total + land_ref[k]
    for copy in stat_copies:
        copy.wait_send()
    for k in range(4):
        whole_ref[k] = total[k : k + 1, :]

    stage_ref[...] = jnp.zeros_like(stage_ref)

    def gradient_of(e, slot):
        def tokens(tile, carry):
            lanes = pl.ds(pl.multiple_of(tile * 128, 128), 128)
            inverse = lax.rsqrt(whole_ref[2 * e, :, lanes] / d_total + EPS)
            factor = whole_ref[2 * e + 1, :, lanes] * inverse * inverse * inverse / d_total
            h = hidden_ref[e, :, lanes].astype(jnp.float32)
            w = cot_ref[e, :, lanes].astype(jnp.float32) * gain_ref[...]
            stage_ref[0:local_d, :] = w * inverse - h * factor
            for gamma in range(parts):
                picked = stage_ref[pl.ds(gamma, row_pad, stride=parts), :]
                gbuf_ref[slot, gamma * row_pad : (gamma + 1) * row_pad, lanes] = picked.astype(jnp.bfloat16)
            return carry

        lax.fori_loop(0, seq // 128, tokens, 0)

    gradient_of(1 - y, 0)
    give = remote(gbuf_ref.at[0], g_ref.at[y], pair_send.at[1], pair_recv.at[1], partner)
    give.start()
    gradient_of(y, 1)
    hold = pltpu.make_async_copy(gbuf_ref.at[1], g_ref.at[y], local_sem.at[1])
    hold.start()

    for step in range(nz - 1):
        for sub in range(2):
            @pl.when(z >= step + 1)
            def _():
                right(step, sub).wait_recv()

            @pl.when(z + step + 1 < nz)
            def _():
                left(step, sub).wait_recv()

            if step + 1 < nz - 1:
                start_both(step + 1, sub)
    for step in range(nz - 1):
        for sub in range(2):

            @pl.when(sends_right(step))
            def _():
                right(step, sub).wait_send()

            @pl.when(sends_left(step))
            def _():
                left(step, sub).wait_send()

    swap.wait_send()
    keep.wait()
    give.wait()
    hold.wait()


def scatter_kernel(n, scale, in_ref, out_ref, land_ref, send_sem, recv_sem):
    me = lax.axis_index("fsdp")
    y = lax.rem(me, 2)
    greet(n, me)
    copies = []
    for k in range(1, n):
        peer = lax.rem(me + k, n)
        copy = remote(in_ref.at[peer], land_ref.at[k - 1], send_sem.at[k - 1], recv_sem.at[k - 1], peer)
        copy.start()
        copies.append(copy)
    totals = [in_ref[me], None]
    for k in range(1, n):
        copies[k - 1].wait()
        value = land_ref[k - 1]
        totals[k % 2] = value if totals[k % 2] is None else totals[k % 2] + value
    out_ref[y] = totals[0] * scale
    out_ref[1 - y] = totals[1] * scale


def on_device(n, hidden_in, cotangent, context, norm_gain, signs_rows, column_sign_flips, kept_index):
    pos = lax.axis_index("fsdp")
    local_d, seq = hidden_in.shape[1:]
    d_total = local_d * n
    rows_a, cols, kept = signs_rows.shape[0], column_sign_flips.shape[0], kept_index.shape[0]
    local_hc = context.shape[1]
    hc = local_hc * n
    local_rows = local_d * hc // cols
    low_rows = local_rows // GROUPS
    parts, segs = cols // SEG, hc // SEG
    deltas = local_d // parts
    row_pad = -(-deltas // 16) * 16
    vmem = pl.BlockSpec(memory_space=pltpu.VMEM)
    smem = pl.BlockSpec(memory_space=pltpu.SMEM)
    anywhere = pl.BlockSpec(memory_space=pl.ANY)
    dma = pltpu.SemaphoreType.DMA
    nz = n // 2

    full_context, g = pl.pallas_call(
        functools.partial(exchange_kernel, n, d_total, row_pad),
        out_shape=(
            jax.ShapeDtypeStruct((nz, 2, local_hc, seq), jnp.bfloat16),
            jax.ShapeDtypeStruct((2, parts * row_pad, seq), jnp.bfloat16),
        ),
        in_specs=[anywhere, anywhere, vmem, anywhere],
        out_specs=(anywhere, anywhere),
        scratch_shapes=[
            pltpu.VMEM(hidden_in.shape, jnp.bfloat16),
            pltpu.VMEM(hidden_in.shape, jnp.bfloat16),
            pltpu.VMEM((8, seq), jnp.float32),
            pltpu.VMEM((4, 1, seq), jnp.float32),
            pltpu.VMEM((n, 8, seq), jnp.float32),
            pltpu.VMEM((parts * row_pad, 128), jnp.float32),
            pltpu.VMEM((2, parts * row_pad, seq), jnp.bfloat16),
            dma((n,)),
            dma((n,)),
            dma((2,)),
            dma((2,)),
            dma((nz - 1, 2)),
            dma((nz - 1, 2)),
            dma((nz - 1, 2)),
            dma((nz - 1, 2)),
            dma((4,)),
        ],
        compiler_params=pltpu.CompilerParams(
            collective_id=1, has_side_effects=True, vmem_limit_bytes=60 * 2**20
        ),
        name="exchange",
    )(hidden_in, cotangent, norm_gain.astype(jnp.float32)[:, None], context)

    sign_b = (1 - 2 * column_sign_flips).astype(jnp.float32)[None, :]
    delta = np.arange(row_pad)
    w = segs * delta[None, :] + np.arange(segs)[:, None]
    live = np.broadcast_to(delta[None, :] < deltas, w.shape).reshape(-1)
    w = np.where(live, w.reshape(-1), 0)
    pair_flips = lax.dynamic_slice_in_dim(signs_rows, (pos // 2) * (2 * local_rows), 2 * local_rows, 0)
    flips = pair_flips.reshape(2, deltas, segs).transpose(0, 2, 1)
    flips = jnp.pad(flips, ((0, 0), (0, 0), (0, row_pad - deltas))).reshape(2, 1, -1)
    sign_a = (1 - 2 * flips).astype(jnp.bfloat16)
    ham = hadamard_np(low_rows)[:, w % low_rows]
    member = (np.arange(HALF)[:, None] == (w // low_rows)[None, :]) & live[None, :]
    l = (ham[:, None, :] * member[None, :, :]).reshape(low_rows * HALF, segs * row_pad)
    l = jnp.asarray(l, jnp.bfloat16)

    span = min(512, kept // n)
    chunks = kept // span
    own = chunks // n
    partial = pl.pallas_call(
        functools.partial(project_kernel, low_rows, cols, span, row_pad),
        out_shape=jax.ShapeDtypeStruct((n, own, span), jnp.float32),
        in_specs=[smem, smem] + [vmem] * 8,
        out_specs=vmem,
        scratch_shapes=[
            pltpu.VMEM((2, segs * row_pad, cols), jnp.bfloat16),
            pltpu.VMEM((low_rows * cols, 2 * HALF), jnp.float32),
            pltpu.VMEM((span, 2 * HALF), jnp.float32),
            pltpu.VMEM((span, 2 * HALF), jnp.float32),
        ],
        compiler_params=pltpu.CompilerParams(vmem_limit_bytes=58 * 2**20),
        name="project",
    )(
        (pos // 2 * 2).reshape(1),
        kept_index,
        kept_index.reshape(chunks, span),
        g,
        full_context.reshape(hc, seq),
        sign_b,
        sign_a,
        l,
        jnp.asarray(hadamard_np(LOW), jnp.bfloat16),
        jnp.eye(2 * HALF, dtype=jnp.bfloat16),
    )
    scale = 1.0 / math.sqrt(rows_a * cols * seq)
    total = pl.pallas_call(
        functools.partial(scatter_kernel, n, scale),
        out_shape=jax.ShapeDtypeStruct((2, own, span), jnp.float32),
        in_specs=[vmem],
        out_specs=vmem,
        scratch_shapes=[pltpu.VMEM((n - 1, own, span), jnp.float32), dma((n - 1,)), dma((n - 1,))],
        compiler_params=pltpu.CompilerParams(collective_id=0, has_side_effects=True),
        name="scatter_sum",
    )(partial)
    return total.reshape(2, own * span)


def solution(mesh):
    return jax.shard_map(
        functools.partial(on_device, mesh.shape["fsdp"]),
        mesh=mesh,
        in_specs=(
            P(("ckpt", "dp"), "fsdp", None),
            P(("ckpt", "dp"), "fsdp", None),
            P(("ckpt", "dp"), "fsdp", None),
            P("fsdp"),
            P(),
            P(),
            P(),
        ),
        out_specs=P(("ckpt", "dp"), "fsdp"),
        check_vma=False,
    )
```

```python
import functools
import math

import jax
import jax.numpy as jnp
import numpy as np
from jax import lax
from jax.experimental import pallas as pl
from jax.experimental.pallas import tpu as pltpu
from jax.sharding import PartitionSpec as P

EPS = 1e-06
GROUPS = 50
HALF = 64
SEG = 512
LOW = 256
NT = (((1,), (1,)), ((), ()))


def hadamard_np(order):
    h = np.ones((1, 1), np.float32)
    while h.shape[0] < order:
        h = np.block([[h, h], [h, -h]])
    return h


def parity(values):
    for shift in (8, 4, 2, 1):
        values = values ^ (values >> shift)
    return values & 1


def dot_nt(a, b):
    return lax.dot_general(a, b, NT, preferred_element_type=jnp.float32)


def project_kernel(
    low_rows, cols, span, row_pad, pos_ref, kept_ref, kept_rows_ref, g_ref, c_in_ref, b_ref, a_ref, l_in_ref, h_ref, eye_ref,
    out_ref, x_ref, table_ref, even_ref, odd_ref, c_ref, l_ref, sem,
):
    segs = c_in_ref.shape[0] // SEG
    parts = cols // SEG
    loads = [
        pltpu.make_async_copy(c_in_ref.at[pl.ds(nb * SEG, SEG)], c_ref.at[pl.ds(nb * SEG, SEG)], sem.at[nb])
        for nb in range(segs)
    ]
    loads.append(pltpu.make_async_copy(l_in_ref, l_ref, sem.at[segs]))
    for load in loads:
        load.start()
    sign_b = (1 - 2 * b_ref[...]).astype(jnp.float32)
    for nb in range(segs):
        loads[nb].wait()
        for e in range(2):
            block = dot_nt(g_ref[e], c_ref[nb * SEG : (nb + 1) * SEG, :])
            for gamma in range(parts):
                omega, sigma = divmod(segs * gamma + nb, parts)
                signed = block[gamma * row_pad : (gamma + 1) * row_pad] * sign_b[:, sigma * SEG : (sigma + 1) * SEG]
                x_ref[e, omega * row_pad : (omega + 1) * row_pad, sigma * SEG : (sigma + 1) * SEG] = signed.astype(
                    jnp.bfloat16
                )
    loads[segs].wait()
    per_step = min(low_rows, 4)
    high = cols // LOW

    def table_step(step, carry):
        start = pl.multiple_of(step * (per_step * HALF), per_step * HALF)
        mixed = []
        for e in range(2):
            left = l_ref[pl.ds(start, per_step * HALF), :] * a_ref[e]
            t = jnp.dot(left, x_ref[e], preferred_element_type=jnp.float32)
            blocks = [t[:, h * LOW : (h + 1) * LOW] for h in range(high)]
            width = 1
            while width < high:
                new = list(blocks)
                for h in range(high):
                    if h & width == 0:
                        new[h] = blocks[h] + blocks[h | width]
                        new[h | width] = blocks[h] - blocks[h | width]
                blocks = new
                width *= 2
            mixed.append([v.astype(jnp.bfloat16) for v in blocks])
        for h in range(high):
            y = jnp.concatenate(
                [mixed[e][h][p * HALF : (p + 1) * HALF] for p in range(per_step) for e in range(2)], axis=0
            )
            r = dot_nt(h_ref[...], y)
            for p in range(per_step):
                row = pl.multiple_of((step * per_step + p) * cols + h * LOW, LOW)
                table_ref[pl.ds(row, LOW), :] = r[:, p * 2 * HALF : (p + 1) * 2 * HALF]
        return carry

    lax.fori_loop(0, low_rows // per_step, table_step, 0)

    shift = (low_rows * cols).bit_length() - 1
    mask = low_rows * cols - 1
    first_group = pos_ref[0] * GROUPS
    own = out_ref.shape[1]
    chunks = kept_rows_ref.shape[0]

    def pick(chunk, buf_ref):
        base = pl.multiple_of(chunk * span, span)
        for u in range(span):
            index = kept_ref[base + u] & mask
            buf_ref[u : u + 1, :] = table_ref[pl.ds(index, 1), :]

    def sign_sum(chunk, buf_ref):
        values = buf_ref[...]
        upper = values.astype(jnp.bfloat16)
        lower = (values - upper.astype(jnp.float32)).astype(jnp.bfloat16)
        turned = dot_nt(eye_ref[...], upper) + dot_nt(eye_ref[...], lower)
        kept_high = kept_rows_ref[pl.ds(chunk, 1), :] >> shift
        lane = lax.broadcasted_iota(jnp.int32, (2 * HALF, span), 0)
        group_index = first_group + jnp.where(lane >= HALF, lane + (GROUPS - HALF), lane)
        sign = (1 - 2 * parity(group_index & kept_high)).astype(jnp.float32)
        out_ref[chunk // own, pl.ds(lax.rem(chunk, own), 1), :] = jnp.sum(turned * sign, axis=0, keepdims=True)

    odd_ref[...] = jnp.zeros_like(odd_ref)

    def pick_step(step, carry):
        pick(2 * step, even_ref)
        sign_sum(lax.max(2 * step - 1, 0), odd_ref)
        pick(2 * step + 1, odd_ref)
        sign_sum(2 * step, even_ref)
        return carry

    lax.fori_loop(0, chunks // 2, pick_step, 0)
    sign_sum(chunks - 1, odd_ref)


def greet(n, me):
    barrier = pltpu.get_barrier_semaphore()
    for k in range(1, n):
        pl.semaphore_signal(
            barrier, inc=1, device_id={"fsdp": lax.rem(me + k, n)}, device_id_type=pl.DeviceIdType.MESH
        )
    pl.semaphore_wait(barrier, n - 1)


def remote(src, dst, send_sem, recv_sem, peer):
    return pltpu.make_async_remote_copy(
        src_ref=src,
        dst_ref=dst,
        send_sem=send_sem,
        recv_sem=recv_sem,
        device_id={"fsdp": peer},
        device_id_type=pl.DeviceIdType.MESH,
    )


def exchange_kernel(
    n, d_total, row_pad, hidden_in_ref, cot_in_ref, gain_ref, context_ref, c_ref, g_ref,
    hidden_ref, cot_ref, stats_ref, whole_ref, land_ref, stage_ref, gbuf_ref,
    stat_send, stat_recv, pair_send, pair_recv, right_send, right_recv, left_send, left_recv, local_sem,
):
    me = lax.axis_index("fsdp")
    y = lax.rem(me, 2)
    z = me // 2
    nz = n // 2
    partner = me + 1 - 2 * y
    local_d, seq = hidden_ref.shape[1:]
    parts = gbuf_ref.shape[1] // row_pad
    reads = [
        pltpu.make_async_copy(hidden_in_ref, hidden_ref, local_sem.at[2]),
        pltpu.make_async_copy(cot_in_ref, cot_ref, local_sem.at[3]),
    ]
    for read in reads:
        read.start()
    greet(n, me)

    def right(step, sub):
        half = y if sub == 0 else 1 - y
        block = lax.max(z - step, 0)
        src = context_ref.at[y] if step == 0 and sub == 0 else c_ref.at[block, half]
        return remote(
            src, c_ref.at[block, half], right_send.at[step, sub], right_recv.at[step, sub], lax.min(me + 2, n - 1)
        )

    def left(step, sub):
        half = y if sub == 0 else 1 - y
        block = lax.min(z + step, nz - 1)
        src = context_ref.at[y] if step == 0 and sub == 0 else c_ref.at[block, half]
        return remote(
            src, c_ref.at[block, half], left_send.at[step, sub], left_recv.at[step, sub], lax.max(me - 2, 0)
        )

    def sends_right(step):
        return jnp.logical_and(z < nz - 1, z >= step)

    def sends_left(step):
        return jnp.logical_and(z > 0, z + step < nz)

    def start_both(step, sub):
        @pl.when(sends_right(step))
        def _():
            right(step, sub).start()

        @pl.when(sends_left(step))
        def _():
            left(step, sub).start()

    swap = remote(context_ref.at[1 - y], c_ref.at[z, y], pair_send.at[0], pair_recv.at[0], partner)
    swap.start()
    start_both(0, 0)
    keep = pltpu.make_async_copy(context_ref.at[y], c_ref.at[z, y], local_sem.at[0])
    keep.start()
    for read in reads:
        read.wait()

    rows = 32

    def add_rows(tile, carry):
        start = pl.multiple_of(tile * rows, rows)
        gain = gain_ref[pl.ds(start, rows), :]
        out = []
        for e in range(2):
            h = hidden_ref[e, pl.ds(start, rows), :].astype(jnp.float32)
            w = cot_ref[e, pl.ds(start, rows), :].astype(jnp.float32) * gain
            out.append(carry[2 * e] + jnp.sum((h * h).reshape(rows // 8, 8, seq), axis=0))
            out.append(carry[2 * e + 1] + jnp.sum((w * h).reshape(rows // 8, 8, seq), axis=0))
        return tuple(out)

    sums = lax.fori_loop(0, local_d // rows, add_rows, (jnp.zeros((8, seq), jnp.float32),) * 4)
    for k in range(4):
        stats_ref[k : k + 1, :] = jnp.sum(sums[k], axis=0, keepdims=True)
    stats_ref[4:8, :] = jnp.zeros((4, seq), jnp.float32)
    stat_copies = []
    for k in range(1, n):
        copy = remote(
            stats_ref, land_ref.at[k], stat_send.at[k], stat_recv.at[k], lax.rem(me + k, n)
        )
        copy.start()
        stat_copies.append(copy)
    swap.wait_recv()
    start_both(0, 1)
    land_ref[0] = stats_ref[...]
    for copy in stat_copies:
        copy.wait_recv()
    total = land_ref[0]
    for k in range(1, n):
        total = total + land_ref[k]
    for copy in stat_copies:
        copy.wait_send()
    for k in range(4):
        whole_ref[k] = total[k : k + 1, :]

    stage_ref[...] = jnp.zeros_like(stage_ref)

    def gradient_of(e, slot):
        def tokens(tile, carry):
            lanes = pl.ds(pl.multiple_of(tile * 128, 128), 128)
            inverse = lax.rsqrt(whole_ref[2 * e, :, lanes] / d_total + EPS)
            factor = whole_ref[2 * e + 1, :, lanes] * inverse * inverse * inverse / d_total
            h = hidden_ref[e, :, lanes].astype(jnp.float32)
            w = cot_ref[e, :, lanes].astype(jnp.float32) * gain_ref[...]
            stage_ref[0:local_d, :] = w * inverse - h * factor
            for gamma in range(parts):
                picked = stage_ref[pl.ds(gamma, row_pad, stride=parts), :]
                gbuf_ref[slot, gamma * row_pad : (gamma + 1) * row_pad, lanes] = picked.astype(jnp.bfloat16)
            return carry

        lax.fori_loop(0, seq // 128, tokens, 0)

    gradient_of(1 - y, 0)
    give = remote(gbuf_ref.at[0], g_ref.at[y], pair_send.at[1], pair_recv.at[1], partner)
    give.start()
    hold = pltpu.make_async_copy(gbuf_ref.at[1], g_ref.at[y], local_sem.at[1])

    for step in range(nz - 1):
        for sub in range(2):
            @pl.when(z >= step + 1)
            def _():
                right(step, sub).wait_recv()

            @pl.when(z + step + 1 < nz)
            def _():
                left(step, sub).wait_recv()

            if step + 1 < nz - 1:
                start_both(step + 1, sub)
            if step == 0 and sub == 0:
                gradient_of(y, 1)
                hold.start()
    for step in range(nz - 1):
        for sub in range(2):

            @pl.when(sends_right(step))
            def _():
                right(step, sub).wait_send()

            @pl.when(sends_left(step))
            def _():
                left(step, sub).wait_send()

    swap.wait_send()
    keep.wait()
    give.wait()
    hold.wait()


def scatter_kernel(n, scale, in_ref, out_ref, land_ref, send_sem, recv_sem):
    me = lax.axis_index("fsdp")
    y = lax.rem(me, 2)
    greet(n, me)
    copies = []
    for k in range(1, n):
        peer = lax.rem(me + k, n)
        copy = remote(in_ref.at[peer], land_ref.at[k - 1], send_sem.at[k - 1], recv_sem.at[k - 1], peer)
        copy.start()
        copies.append(copy)
    totals = [in_ref[me], None]
    for k in range(1, n):
        copies[k - 1].wait()
        value = land_ref[k - 1]
        totals[k % 2] = value if totals[k % 2] is None else totals[k % 2] + value
    out_ref[y] = totals[0] * scale
    out_ref[1 - y] = totals[1] * scale


def on_device(n, hidden_in, cotangent, context, norm_gain, signs_rows, column_sign_flips, kept_index):
    pos = lax.axis_index("fsdp")
    local_d, seq = hidden_in.shape[1:]
    d_total = local_d * n
    rows_a, cols, kept = signs_rows.shape[0], column_sign_flips.shape[0], kept_index.shape[0]
    local_hc = context.shape[1]
    hc = local_hc * n
    local_rows = local_d * hc // cols
    low_rows = local_rows // GROUPS
    parts, segs = cols // SEG, hc // SEG
    deltas = local_d // parts
    row_pad = -(-deltas // 16) * 16
    vmem = pl.BlockSpec(memory_space=pltpu.VMEM)
    smem = pl.BlockSpec(memory_space=pltpu.SMEM)
    anywhere = pl.BlockSpec(memory_space=pl.ANY)
    dma = pltpu.SemaphoreType.DMA
    nz = n // 2

    full_context, g = pl.pallas_call(
        functools.partial(exchange_kernel, n, d_total, row_pad),
        out_shape=(
            jax.ShapeDtypeStruct((nz, 2, local_hc, seq), jnp.bfloat16),
            jax.ShapeDtypeStruct((2, parts * row_pad, seq), jnp.bfloat16),
        ),
        in_specs=[anywhere, anywhere, vmem, anywhere],
        out_specs=(anywhere, anywhere),
        scratch_shapes=[
            pltpu.VMEM(hidden_in.shape, jnp.bfloat16),
            pltpu.VMEM(hidden_in.shape, jnp.bfloat16),
            pltpu.VMEM((8, seq), jnp.float32),
            pltpu.VMEM((4, 1, seq), jnp.float32),
            pltpu.VMEM((n, 8, seq), jnp.float32),
            pltpu.VMEM((parts * row_pad, 128), jnp.float32),
            pltpu.VMEM((2, parts * row_pad, seq), jnp.bfloat16),
            dma((n,)),
            dma((n,)),
            dma((2,)),
            dma((2,)),
            dma((nz - 1, 2)),
            dma((nz - 1, 2)),
            dma((nz - 1, 2)),
            dma((nz - 1, 2)),
            dma((4,)),
        ],
        compiler_params=pltpu.CompilerParams(
            collective_id=1, has_side_effects=True, vmem_limit_bytes=60 * 2**20
        ),
        name="exchange",
    )(hidden_in, cotangent, norm_gain.astype(jnp.float32)[:, None], context)

    delta = np.arange(row_pad)
    w = segs * delta[None, :] + np.arange(segs)[:, None]
    live = np.broadcast_to(delta[None, :] < deltas, w.shape).reshape(-1)
    w = np.where(live, w.reshape(-1), 0)
    pair_flips = lax.dynamic_slice_in_dim(signs_rows, (pos // 2) * (2 * local_rows), 2 * local_rows, 0)
    flips = pair_flips.reshape(2, deltas, segs).transpose(0, 2, 1)
    flips = jnp.pad(flips, ((0, 0), (0, 0), (0, row_pad - deltas))).reshape(2, 1, -1)
    sign_a = (1 - 2 * flips).astype(jnp.bfloat16)
    ham = hadamard_np(low_rows)[:, w % low_rows]
    member = (np.arange(HALF)[:, None] == (w // low_rows)[None, :]) & live[None, :]
    l = (ham[:, None, :] * member[None, :, :]).reshape(low_rows * HALF, segs * row_pad)
    l = jnp.asarray(l, jnp.bfloat16)

    span = min(512, kept // n)
    chunks = kept // span
    own = chunks // n
    partial = pl.pallas_call(
        functools.partial(project_kernel, low_rows, cols, span, row_pad),
        out_shape=jax.ShapeDtypeStruct((n, own, span), jnp.float32),
        in_specs=[smem, smem, vmem, vmem, anywhere, vmem, vmem, anywhere, vmem, vmem],
        out_specs=vmem,
        scratch_shapes=[
            pltpu.VMEM((2, segs * row_pad, cols), jnp.bfloat16),
            pltpu.VMEM((low_rows * cols, 2 * HALF), jnp.float32),
            pltpu.VMEM((span, 2 * HALF), jnp.float32),
            pltpu.VMEM((span, 2 * HALF), jnp.float32),
            pltpu.VMEM((hc, seq), jnp.bfloat16),
            pltpu.VMEM(l.shape, jnp.bfloat16),
            dma((segs + 1,)),
        ],
        compiler_params=pltpu.CompilerParams(vmem_limit_bytes=58 * 2**20),
        name="project",
    )(
        (pos // 2 * 2).reshape(1),
        kept_index,
        kept_index.reshape(chunks, span),
        g,
        full_context.reshape(hc, seq),
        column_sign_flips[None, :],
        sign_a,
        l,
        jnp.asarray(hadamard_np(LOW), jnp.bfloat16),
        jnp.asarray(np.eye(2 * HALF), jnp.bfloat16),
    )
    scale = 1.0 / math.sqrt(rows_a * cols * seq)
    total = pl.pallas_call(
        functools.partial(scatter_kernel, n, scale),
        out_shape=jax.ShapeDtypeStruct((2, own, span), jnp.float32),
        in_specs=[vmem],
        out_specs=vmem,
        scratch_shapes=[pltpu.VMEM((n - 1, own, span), jnp.float32), dma((n - 1,)), dma((n - 1,))],
        compiler_params=pltpu.CompilerParams(collective_id=0, has_side_effects=True),
        name="scatter_sum",
    )(partial)
    return total.reshape(2, own * span)


def solution(mesh):
    return jax.shard_map(
        functools.partial(on_device, mesh.shape["fsdp"]),
        mesh=mesh,
        in_specs=(
            P(("ckpt", "dp"), "fsdp", None),
            P(("ckpt", "dp"), "fsdp", None),
            P(("ckpt", "dp"), "fsdp", None),
            P("fsdp"),
            P(),
            P(),
            P(),
        ),
        out_specs=P(("ckpt", "dp"), "fsdp"),
        check_vma=False,
    )
```

```python
import functools
import math

import jax
import jax.numpy as jnp
import numpy as np
from jax import lax
from jax.experimental import pallas as pl
from jax.experimental.pallas import tpu as pltpu
from jax.sharding import PartitionSpec as P

EPS = 1e-06
GROUPS = 50
HALF = 64
SEG = 512
LOW = 256
NT = (((1,), (1,)), ((), ()))


def hadamard_np(order):
    h = np.ones((1, 1), np.float32)
    while h.shape[0] < order:
        h = np.block([[h, h], [h, -h]])
    return h


def parity(values):
    for shift in (8, 4, 2, 1):
        values = values ^ (values >> shift)
    return values & 1


def dot_nt(a, b):
    return lax.dot_general(a, b, NT, preferred_element_type=jnp.float32)


def project_kernel(
    low_rows, cols, span, row_pad, pos_ref, kept_ref, kept_rows_ref, g_ref, c_in_ref, b_ref, a_ref, l_in_ref, h_ref, eye_ref,
    out_ref, x_ref, table_ref, even_ref, odd_ref, c_ref, l_ref, sem,
):
    segs = c_in_ref.shape[0] // SEG
    parts = cols // SEG
    loads = [
        pltpu.make_async_copy(c_in_ref.at[pl.ds(nb * SEG, SEG)], c_ref.at[pl.ds(nb * SEG, SEG)], sem.at[nb])
        for nb in range(segs)
    ]
    loads.append(pltpu.make_async_copy(l_in_ref, l_ref, sem.at[segs]))
    for load in loads:
        load.start()
    sign_b = (1 - 2 * b_ref[...]).astype(jnp.float32)
    for nb in range(segs):
        loads[nb].wait()
        for e in range(2):
            block = dot_nt(g_ref[e], c_ref[nb * SEG : (nb + 1) * SEG, :])
            for gamma in range(parts):
                omega, sigma = divmod(segs * gamma + nb, parts)
                signed = block[gamma * row_pad : (gamma + 1) * row_pad] * sign_b[:, sigma * SEG : (sigma + 1) * SEG]
                x_ref[e, omega * row_pad : (omega + 1) * row_pad, sigma * SEG : (sigma + 1) * SEG] = signed.astype(
                    jnp.bfloat16
                )
    loads[segs].wait()
    per_step = min(low_rows, 4)
    high = cols // LOW

    def table_step(step, carry):
        start = pl.multiple_of(step * (per_step * HALF), per_step * HALF)
        mixed = []
        for e in range(2):
            left = l_ref[pl.ds(start, per_step * HALF), :] * a_ref[e]
            t = jnp.dot(left, x_ref[e], preferred_element_type=jnp.float32)
            blocks = [t[:, h * LOW : (h + 1) * LOW] for h in range(high)]
            width = 1
            while width < high:
                new = list(blocks)
                for h in range(high):
                    if h & width == 0:
                        new[h] = blocks[h] + blocks[h | width]
                        new[h | width] = blocks[h] - blocks[h | width]
                blocks = new
                width *= 2
            mixed.append([v.astype(jnp.bfloat16) for v in blocks])
        for h in range(high):
            y = jnp.concatenate(
                [mixed[e][h][p * HALF : (p + 1) * HALF] for p in range(per_step) for e in range(2)], axis=0
            )
            r = dot_nt(h_ref[...], y)
            for p in range(per_step):
                row = pl.multiple_of((step * per_step + p) * cols + h * LOW, LOW)
                table_ref[pl.ds(row, LOW), :] = r[:, p * 2 * HALF : (p + 1) * 2 * HALF]
        return carry

    lax.fori_loop(0, low_rows // per_step, table_step, 0)

    shift = (low_rows * cols).bit_length() - 1
    first_group = pos_ref[0] * GROUPS
    own = out_ref.shape[1]
    chunks = kept_rows_ref.shape[0]

    def pick(chunk, buf_ref):
        base = pl.multiple_of(chunk * span, span)
        for u in range(span):
            index = kept_ref[base + u]
            buf_ref[u : u + 1, :] = table_ref[pl.ds(index, 1), :]

    def sign_sum(chunk, buf_ref):
        values = buf_ref[...]
        upper = values.astype(jnp.bfloat16)
        lower = (values - upper.astype(jnp.float32)).astype(jnp.bfloat16)
        turned = dot_nt(eye_ref[...], upper) + dot_nt(eye_ref[...], lower)
        kept_high = kept_rows_ref[pl.ds(chunk, 1), :] >> shift
        lane = lax.broadcasted_iota(jnp.int32, (2 * HALF, span), 0)
        group_index = first_group + jnp.where(lane >= HALF, lane + (GROUPS - HALF), lane)
        sign = (1 - 2 * parity(group_index & kept_high)).astype(jnp.float32)
        out_ref[chunk // own, pl.ds(lax.rem(chunk, own), 1), :] = jnp.sum(turned * sign, axis=0, keepdims=True)

    odd_ref[...] = jnp.zeros_like(odd_ref)

    def pick_step(step, carry):
        pick(2 * step, even_ref)
        sign_sum(lax.max(2 * step - 1, 0), odd_ref)
        pick(2 * step + 1, odd_ref)
        sign_sum(2 * step, even_ref)
        return carry

    lax.fori_loop(0, chunks // 2, pick_step, 0)
    sign_sum(chunks - 1, odd_ref)


def greet(n, me):
    barrier = pltpu.get_barrier_semaphore()
    for k in range(1, n):
        pl.semaphore_signal(
            barrier, inc=1, device_id={"fsdp": lax.rem(me + k, n)}, device_id_type=pl.DeviceIdType.MESH
        )
    pl.semaphore_wait(barrier, n - 1)


def remote(src, dst, send_sem, recv_sem, peer):
    return pltpu.make_async_remote_copy(
        src_ref=src,
        dst_ref=dst,
        send_sem=send_sem,
        recv_sem=recv_sem,
        device_id={"fsdp": peer},
        device_id_type=pl.DeviceIdType.MESH,
    )


def exchange_kernel(
    n, d_total, row_pad, hidden_in_ref, cot_in_ref, gain_ref, context_ref, c_ref, g_ref,
    hidden_ref, cot_ref, stats_ref, whole_ref, land_ref, stage_ref, gbuf_ref,
    stat_send, stat_recv, pair_send, pair_recv, right_send, right_recv, left_send, left_recv, local_sem,
):
    me = lax.axis_index("fsdp")
    y = lax.rem(me, 2)
    z = me // 2
    nz = n // 2
    partner = me + 1 - 2 * y
    local_d, seq = hidden_ref.shape[1:]
    parts = gbuf_ref.shape[1] // row_pad
    reads = [
        pltpu.make_async_copy(hidden_in_ref, hidden_ref, local_sem.at[2]),
        pltpu.make_async_copy(cot_in_ref, cot_ref, local_sem.at[3]),
    ]
    for read in reads:
        read.start()
    greet(n, me)

    def right(step, sub):
        half = y if sub == 0 else 1 - y
        block = lax.max(z - step, 0)
        src = context_ref.at[y] if step == 0 and sub == 0 else c_ref.at[block, half]
        return remote(
            src, c_ref.at[block, half], right_send.at[step, sub], right_recv.at[step, sub], lax.min(me + 2, n - 1)
        )

    def left(step, sub):
        half = y if sub == 0 else 1 - y
        block = lax.min(z + step, nz - 1)
        src = context_ref.at[y] if step == 0 and sub == 0 else c_ref.at[block, half]
        return remote(
            src, c_ref.at[block, half], left_send.at[step, sub], left_recv.at[step, sub], lax.max(me - 2, 0)
        )

    def sends_right(step):
        return jnp.logical_and(z < nz - 1, z >= step)

    def sends_left(step):
        return jnp.logical_and(z > 0, z + step < nz)

    def start_both(step, sub):
        @pl.when(sends_right(step))
        def _():
            right(step, sub).start()

        @pl.when(sends_left(step))
        def _():
            left(step, sub).start()

    swap = remote(context_ref.at[1 - y], c_ref.at[z, y], pair_send.at[0], pair_recv.at[0], partner)
    swap.start()
    start_both(0, 0)
    keep = pltpu.make_async_copy(context_ref.at[y], c_ref.at[z, y], local_sem.at[0])
    keep.start()
    for read in reads:
        read.wait()

    rows = 32

    def add_rows(tile, carry):
        start = pl.multiple_of(tile * rows, rows)
        gain = gain_ref[pl.ds(start, rows), :]
        out = []
        for e in range(2):
            h = hidden_ref[e, pl.ds(start, rows), :].astype(jnp.float32)
            w = cot_ref[e, pl.ds(start, rows), :].astype(jnp.float32) * gain
            out.append(carry[2 * e] + jnp.sum((h * h).reshape(rows // 8, 8, seq), axis=0))
            out.append(carry[2 * e + 1] + jnp.sum((w * h).reshape(rows // 8, 8, seq), axis=0))
        return tuple(out)

    sums = lax.fori_loop(0, local_d // rows, add_rows, (jnp.zeros((8, seq), jnp.float32),) * 4)
    for k in range(4):
        stats_ref[k : k + 1, :] = jnp.sum(sums[k], axis=0, keepdims=True)
    stats_ref[4:8, :] = jnp.zeros((4, seq), jnp.float32)
    stat_copies = []
    for k in range(1, n):
        copy = remote(
            stats_ref, land_ref.at[k], stat_send.at[k], stat_recv.at[k], lax.rem(me + k, n)
        )
        copy.start()
        stat_copies.append(copy)
    swap.wait_recv()
    start_both(0, 1)
    land_ref[0] = stats_ref[...]
    for copy in stat_copies:
        copy.wait_recv()
    total = land_ref[0]
    for k in range(1, n):
        total = total + land_ref[k]
    for copy in stat_copies:
        copy.wait_send()
    for k in range(4):
        whole_ref[k] = total[k : k + 1, :]

    stage_ref[...] = jnp.zeros_like(stage_ref)

    def gradient_of(e, slot):
        def tokens(tile, carry):
            lanes = pl.ds(pl.multiple_of(tile * 128, 128), 128)
            inverse = lax.rsqrt(whole_ref[2 * e, :, lanes] / d_total + EPS)
            factor = whole_ref[2 * e + 1, :, lanes] * inverse * inverse * inverse / d_total
            h = hidden_ref[e, :, lanes].astype(jnp.float32)
            w = cot_ref[e, :, lanes].astype(jnp.float32) * gain_ref[...]
            stage_ref[0:local_d, :] = w * inverse - h * factor
            for gamma in range(parts):
                picked = stage_ref[pl.ds(gamma, row_pad, stride=parts), :]
                gbuf_ref[slot, gamma * row_pad : (gamma + 1) * row_pad, lanes] = picked.astype(jnp.bfloat16)
            return carry

        lax.fori_loop(0, seq // 128, tokens, 0)

    gradient_of(1 - y, 0)
    give = remote(gbuf_ref.at[0], g_ref.at[y], pair_send.at[1], pair_recv.at[1], partner)
    give.start()
    hold = pltpu.make_async_copy(gbuf_ref.at[1], g_ref.at[y], local_sem.at[1])

    for step in range(nz - 1):
        for sub in range(2):
            @pl.when(z >= step + 1)
            def _():
                right(step, sub).wait_recv()

            @pl.when(z + step + 1 < nz)
            def _():
                left(step, sub).wait_recv()

            if step + 1 < nz - 1:
                start_both(step + 1, sub)
            if step == 0 and sub == 0:
                gradient_of(y, 1)
                hold.start()
    for step in range(nz - 1):
        for sub in range(2):

            @pl.when(sends_right(step))
            def _():
                right(step, sub).wait_send()

            @pl.when(sends_left(step))
            def _():
                left(step, sub).wait_send()

    swap.wait_send()
    keep.wait()
    give.wait()
    hold.wait()


def scatter_kernel(n, scale, in_ref, out_ref, land_ref, send_sem, recv_sem):
    me = lax.axis_index("fsdp")
    y = lax.rem(me, 2)
    greet(n, me)
    copies = []
    for k in range(1, n):
        peer = lax.rem(me + k, n)
        copy = remote(in_ref.at[peer], land_ref.at[k - 1], send_sem.at[k - 1], recv_sem.at[k - 1], peer)
        copy.start()
        copies.append(copy)
    totals = [in_ref[me], None]
    for k in range(1, n):
        copies[k - 1].wait()
        value = land_ref[k - 1]
        totals[k % 2] = value if totals[k % 2] is None else totals[k % 2] + value
    out_ref[y] = totals[0] * scale
    out_ref[1 - y] = totals[1] * scale


def on_device(n, hidden_in, cotangent, context, norm_gain, signs_rows, column_sign_flips, kept_index):
    pos = lax.axis_index("fsdp")
    local_d, seq = hidden_in.shape[1:]
    d_total = local_d * n
    rows_a, cols, kept = signs_rows.shape[0], column_sign_flips.shape[0], kept_index.shape[0]
    local_hc = context.shape[1]
    hc = local_hc * n
    local_rows = local_d * hc // cols
    low_rows = local_rows // GROUPS
    parts, segs = cols // SEG, hc // SEG
    deltas = local_d // parts
    row_pad = -(-deltas // 16) * 16
    vmem = pl.BlockSpec(memory_space=pltpu.VMEM)
    smem = pl.BlockSpec(memory_space=pltpu.SMEM)
    anywhere = pl.BlockSpec(memory_space=pl.ANY)
    dma = pltpu.SemaphoreType.DMA
    nz = n // 2

    full_context, g = pl.pallas_call(
        functools.partial(exchange_kernel, n, d_total, row_pad),
        out_shape=(
            jax.ShapeDtypeStruct((nz, 2, local_hc, seq), jnp.bfloat16),
            jax.ShapeDtypeStruct((2, parts * row_pad, seq), jnp.bfloat16),
        ),
        in_specs=[anywhere, anywhere, vmem, anywhere],
        out_specs=(anywhere, anywhere),
        scratch_shapes=[
            pltpu.VMEM(hidden_in.shape, jnp.bfloat16),
            pltpu.VMEM(hidden_in.shape, jnp.bfloat16),
            pltpu.VMEM((8, seq), jnp.float32),
            pltpu.VMEM((4, 1, seq), jnp.float32),
            pltpu.VMEM((n, 8, seq), jnp.float32),
            pltpu.VMEM((parts * row_pad, 128), jnp.float32),
            pltpu.VMEM((2, parts * row_pad, seq), jnp.bfloat16),
            dma((n,)),
            dma((n,)),
            dma((2,)),
            dma((2,)),
            dma((nz - 1, 2)),
            dma((nz - 1, 2)),
            dma((nz - 1, 2)),
            dma((nz - 1, 2)),
            dma((4,)),
        ],
        compiler_params=pltpu.CompilerParams(
            collective_id=1, has_side_effects=True, vmem_limit_bytes=60 * 2**20
        ),
        name="exchange",
    )(hidden_in, cotangent, norm_gain.astype(jnp.float32)[:, None], context)

    delta = np.arange(row_pad)
    w = segs * delta[None, :] + np.arange(segs)[:, None]
    live = np.broadcast_to(delta[None, :] < deltas, w.shape).reshape(-1)
    w = np.where(live, w.reshape(-1), 0)
    pair_flips = lax.dynamic_slice_in_dim(signs_rows, (pos // 2) * (2 * local_rows), 2 * local_rows, 0)
    flips = pair_flips.reshape(2, deltas, segs).transpose(0, 2, 1)
    flips = jnp.pad(flips, ((0, 0), (0, 0), (0, row_pad - deltas))).reshape(2, 1, -1)
    sign_a = (1 - 2 * flips).astype(jnp.bfloat16)
    ham = hadamard_np(low_rows)[:, w % low_rows]
    member = (np.arange(HALF)[:, None] == (w // low_rows)[None, :]) & live[None, :]
    l = (ham[:, None, :] * member[None, :, :]).reshape(low_rows * HALF, segs * row_pad)
    l = jnp.asarray(l, jnp.bfloat16)

    span = min(512, kept // n)
    chunks = kept // span
    own = chunks // n
    partial = pl.pallas_call(
        functools.partial(project_kernel, low_rows, cols, span, row_pad),
        out_shape=jax.ShapeDtypeStruct((n, own, span), jnp.float32),
        in_specs=[smem, smem, vmem, vmem, anywhere, vmem, vmem, anywhere, vmem, vmem],
        out_specs=vmem,
        scratch_shapes=[
            pltpu.VMEM((2, segs * row_pad, cols), jnp.bfloat16),
            pltpu.VMEM((low_rows * cols, 2 * HALF), jnp.float32),
            pltpu.VMEM((span, 2 * HALF), jnp.float32),
            pltpu.VMEM((span, 2 * HALF), jnp.float32),
            pltpu.VMEM((hc, seq), jnp.bfloat16),
            pltpu.VMEM(l.shape, jnp.bfloat16),
            dma((segs + 1,)),
        ],
        compiler_params=pltpu.CompilerParams(vmem_limit_bytes=58 * 2**20),
        name="project",
    )(
        (pos // 2 * 2).reshape(1),
        kept_index & (low_rows * cols - 1),
        kept_index.reshape(chunks, span),
        g,
        full_context.reshape(hc, seq),
        column_sign_flips[None, :],
        sign_a,
        l,
        jnp.asarray(hadamard_np(LOW), jnp.bfloat16),
        jnp.asarray(np.eye(2 * HALF), jnp.bfloat16),
    )
    scale = 1.0 / math.sqrt(rows_a * cols * seq)
    total = pl.pallas_call(
        functools.partial(scatter_kernel, n, scale),
        out_shape=jax.ShapeDtypeStruct((2, own, span), jnp.float32),
        in_specs=[vmem],
        out_specs=vmem,
        scratch_shapes=[pltpu.VMEM((n - 1, own, span), jnp.float32), dma((n - 1,)), dma((n - 1,))],
        compiler_params=pltpu.CompilerParams(collective_id=0, has_side_effects=True),
        name="scatter_sum",
    )(partial)
    return total.reshape(2, own * span)


def solution(mesh):
    return jax.shard_map(
        functools.partial(on_device, mesh.shape["fsdp"]),
        mesh=mesh,
        in_specs=(
            P(("ckpt", "dp"), "fsdp", None),
            P(("ckpt", "dp"), "fsdp", None),
            P(("ckpt", "dp"), "fsdp", None),
            P("fsdp"),
            P(),
            P(),
            P(),
        ),
        out_specs=P(("ckpt", "dp"), "fsdp"),
        check_vma=False,
    )
```
